32 devices in a mesh: groups: 2 (over x), tp: 8 (over z, y), sub: 2 (over core).
Axes of the slice: x: 2, y: 2, z: 4, core: 2. Of those that a mesh axis runs over, the one named last changes fastest.
Arguments:
- queries: bfloat16 [4096, 12288], P(('groups', 'tp', 'sub')), parts along dimension 0, may hold values from -68 to 68
- new_kv: bfloat16 [4096, 2048], P(('groups', 'tp', 'sub')), parts along dimension 0, may hold values from -6 to 6
- prefix_kv: bfloat16 [4, 4096, 2048], P('groups', 'tp'), parts along dimension 0, may hold values from -6 to 6
- prefix_len: int32 [4], P('groups'), parts along dimension 0, may hold values from 1 to 4096, as said below
- owner: int32 [4096], P(('groups', 'tp', 'sub')), parts along dimension 0, may hold values from 0 to 15, as said below
- slot: int32 [4096], P(('groups', 'tp', 'sub')), parts along dimension 0, may hold values from 0 to 127, as said below
Outputs:
- attended: bfloat16 [4096, 12288], P(('groups', 'tp', 'sub')), parts along dimension 0
- pages: bfloat16 [4096, 2048], P(('groups', 'tp', 'sub')), parts along dimension 0
The draws below stay inside these ranges and needn't reach their ends.
There are 2 independent parts, one for each index of `groups`. The reference program is written for one: setup_inputs(seed, part) draws one part's arguments, and reference() takes and returns one part's arrays. A program takes and returns all parts, laid end to end along the dimension named above; each array names one. Nothing has to cross between parts.
Inputs may be any that keep to these rules, and one draw needn't show every extreme that they name: One prompt in each draw has prefix_len 4096. Among the 128 rows of one device (aligned blocks) at most 9 name the same owner, and in every such block one owner is named by exactly 9 rows; every owner is named by exactly 128 rows in all. The pair (owner, slot) differs from row to row, so every page slot is written once.
All inputs are finite; a program needn't handle non-finite values.
Results may differ from the reference program's by a relative error of at most 0.0049.
Values may be sent and summed in bfloat16 or wider, within the bound.
A program may use at most 128 MiB of HBM per device.

```python
import jax
import jax.numpy as jnp
from jax import lax

HEADS = 96
KVH = 8
HS = 128
SPAN = 1024
NP = 2
PMAX = 4096
NEW = 2048
NDEV = 16
ROWS_SRC = 128
RMAX = 9


def owner_plan(key):
    key_a, key_b, key_c, key_d = jax.random.split(key, 4)
    sigma = jax.random.permutation(key_a, NDEV)
    tau = jax.random.permutation(key_b, NDEV)
    tau_back = jnp.argsort(tau, stable=True)
    relabel = jax.random.permutation(key_c, NDEV)
    spots = jnp.arange(ROWS_SRC)
    spare = max(ROWS_SRC - RMAX, 1)
    offset = jnp.where(spots < RMAX, 0, 1 + (spots - RMAX) * (NDEV - 1) // spare)
    labels = relabel[offset]
    row_keys = jax.random.split(key_d, NDEV)
    positions = jax.vmap(lambda one_key: jax.random.permutation(one_key, ROWS_SRC))(row_keys)
    target = (sigma[:, None] + labels[positions]) % NDEV
    owners = tau_back[target]
    return (owners.reshape(-1).astype(jnp.int32), positions.reshape(-1).astype(jnp.int32))


def draw_owner(key, part):
    return owner_plan(key)[0]


def draw_slot(key, part):
    return owner_plan(key)[1]


def draw_prefix_len(key, part):
    key = jax.random.fold_in(key, 5)
    key_a, key_b = jax.random.split(key)
    lengths = jax.random.randint(key_a, (NP,), 1, PMAX + 1)
    longest = jax.random.randint(key_b, (), 0, NP)
    return jnp.where(jnp.arange(NP) == longest, PMAX, lengths).astype(jnp.int32)


def draw_queries(key, part):
    key = jax.random.fold_in(key, 11)
    key_a = jax.random.fold_in(key, 0)
    shape = (NEW, HEADS * HS)
    values = jnp.clip(jax.random.normal(key_a, shape, jnp.float32), -6.0, 6.0)
    return values.astype(jnp.bfloat16)


def block_levels(key, extent, cuts, low, high):
    gain = 1.0
    for position, blocks in cuts:
        heights = jax.random.uniform(jax.random.fold_in(jax.random.fold_in(key, 6), position), (blocks,), jnp.float32, low / len(cuts), high / len(cuts))
        gain = gain * jnp.repeat(jnp.exp(heights), extent[position] // blocks).reshape((-1,) + (1,) * (len(extent) - 1 - position))
    return gain


def noise(own_key, extent, width, bound, cuts=(), held_as=jnp.bfloat16):
    gain = block_levels(own_key, extent, cuts, -0.22, 0.18) if cuts else 1.0
    entries = jax.random.normal(own_key, extent, jnp.float32) * width * gain
    return jnp.minimum(jnp.maximum(entries, -bound), bound).astype(held_as)


def setup_inputs(seed: int = 0, part: int = 0) -> dict:
    key_list = jax.random.split(jax.random.key(seed), 7)
    part_keys = jax.random.split(jax.random.fold_in(key_list[6], part), 7)
    queries = draw_queries(jax.random.fold_in(jax.random.fold_in(key_list[6], part), 71), part)
    new_kv = noise(part_keys[1], (NEW, 2 * KVH * HS), 1.0, 6.0, ((0, 16),))
    prefix_kv = noise(part_keys[2], (NP, PMAX, 2 * KVH * HS), 1.0, 6.0, ((1, 8),))
    prefix_len = draw_prefix_len(jax.random.fold_in(jax.random.fold_in(key_list[6], part), 71), part)
    owner = draw_owner(jax.random.fold_in(jax.random.fold_in(key_list[6], part), 71), part)
    slot = draw_slot(jax.random.fold_in(jax.random.fold_in(key_list[6], part), 71), part)
    return dict(queries=queries, new_kv=new_kv, prefix_kv=prefix_kv, prefix_len=prefix_len, owner=owner, slot=slot)


def softmax_mix(query_head, key_head, value_head, allowed, score_scale):
    scores = jnp.dot(query_head, key_head.T, preferred_element_type=jnp.float32) * score_scale
    scores = jnp.where(allowed, scores, -1e30)
    top_score = jnp.max(scores, axis=1, keepdims=True)
    expo = jnp.where(allowed, jnp.exp(scores - top_score), 0.0)
    total = jnp.sum(expo, axis=1, keepdims=True)
    weights = (expo / total).astype(jnp.bfloat16)
    return jnp.dot(weights, value_head, preferred_element_type=jnp.float32).astype(jnp.bfloat16)


def reference(queries, new_kv, prefix_kv, prefix_len, owner, slot):
    score_scale = HS ** -0.5
    group_size = HEADS // KVH
    query_blocks = queries.reshape(NP, SPAN, HEADS, HS)
    new_blocks = new_kv.reshape(NP, SPAN, 2, KVH, HS)
    cached = prefix_kv.reshape(NP, PMAX, 2, KVH, HS)
    column = jnp.arange(PMAX + SPAN)
    span_pos = jnp.arange(SPAN)

    def prompt(packed):
        query_rows, new_rows, cache_rows, length = packed
        key_rows = jnp.concatenate([cache_rows[:, 0], new_rows[:, 0]], axis=0)
        value_rows = jnp.concatenate([cache_rows[:, 1], new_rows[:, 1]], axis=0)
        allowed = jnp.where(column[None, :] < PMAX, column[None, :] < length,
                            column[None, :] - PMAX <= span_pos[:, None])

        def one_head(head_id):
            kv_head = head_id // group_size
            query_head = lax.dynamic_index_in_dim(query_rows, head_id, 1, keepdims=False)
            key_head = lax.dynamic_index_in_dim(key_rows, kv_head, 1, keepdims=False)
            value_head = lax.dynamic_index_in_dim(value_rows, kv_head, 1, keepdims=False)
            return softmax_mix(query_head, key_head, value_head, allowed, score_scale)

        mixed = lax.map(one_head, jnp.arange(HEADS))
        return jnp.transpose(mixed, (1, 0, 2)).reshape(SPAN, HEADS * HS)

    attended = lax.map(prompt, (query_blocks, new_blocks, cached, prefix_len)).reshape(NEW, HEADS * HS)
    target = owner * ROWS_SRC + slot
    pages = jnp.zeros((NEW, 2 * KVH * HS), jnp.bfloat16).at[target].set(new_kv)
    return attended, pages
```

```python
import jax
import jax.numpy as jnp
import numpy as np
from jax import lax
from jax.experimental import pallas as pl
from jax.experimental.pallas import tpu as pltpu
from jax.sharding import PartitionSpec as P

HEADS = 96
KVH = 8
HS = 128
SPAN = 1024
PMAX = 4096


def softmax_mix(query_head, key_head, value_head, allowed, score_scale):
    scores = jnp.dot(query_head, key_head.T, preferred_element_type=jnp.float32) * score_scale
    scores = jnp.where(allowed, scores, -1e30)
    top_score = jnp.max(scores, axis=1, keepdims=True)
    expo = jnp.where(allowed, jnp.exp(scores - top_score), 0.0)
    total = jnp.sum(expo, axis=1, keepdims=True)
    weights = (expo / total).astype(jnp.bfloat16)
    return jnp.dot(weights, value_head, preferred_element_type=jnp.float32).astype(jnp.bfloat16)


def shards(queries, new_kv, prefix_kv, prefix_len, owner, slot):
    tp_count = lax.axis_size("tp")
    sub_count = lax.axis_size("sub")
    sub_index = lax.axis_index("sub")
    dev_count = tp_count * sub_count
    rows_src = queries.shape[0]
    prompts = prefix_len.shape[0]
    heads_dev = HEADS // tp_count
    group_size = HEADS // KVH
    score_scale = HS ** (-0.5)
    head_of_peer = np.arange(tp_count) * heads_dev // group_size
    kv_local = new_kv.reshape(rows_src, 2, KVH, HS)
    query_send = queries.reshape(rows_src, tp_count, heads_dev * HS)
    query_recv = lax.all_to_all(query_send, "tp", split_axis=1, concat_axis=0, tiled=True)
    dest_heads = np.repeat(head_of_peer, sub_count)
    key_send = jnp.take(kv_local, dest_heads, axis=2)
    key_send = jnp.transpose(key_send, (2, 0, 1, 3)).reshape(dev_count, rows_src, 2 * HS)
    new_keys = lax.all_to_all(
        key_send, ("tp", "sub"), split_axis=0, concat_axis=0, tiled=True
    ).reshape(-1, 2 * HS)
    shard_rows = prefix_kv.shape[1]
    cache_local = prefix_kv.reshape(prompts, shard_rows, 2, KVH, HS)
    prefix_send = jnp.take(cache_local, head_of_peer, axis=3)
    prefix_send = jnp.transpose(prefix_send, (0, 3, 1, 2, 4)).reshape(
        prompts, tp_count, shard_rows, 2 * HS
    )
    cached = lax.all_to_all(prefix_send, "tp", split_axis=1, concat_axis=1, tiled=True)
    cached = cached.reshape(prompts, PMAX, 2, HS)
    local_rows = tp_count * rows_src
    query_rows_all = local_rows // prompts
    arrival = jnp.arange(local_rows)
    global_row = (arrival // rows_src * sub_count + sub_index) * rows_src + arrival % rows_src
    query_pos = (global_row % SPAN).reshape(prompts, query_rows_all)
    query_blocks = query_recv.reshape(prompts, query_rows_all, heads_dev, HS)
    new_blocks = new_keys.reshape(prompts, SPAN, 2, HS)
    column = jnp.arange(PMAX + SPAN)

    def prompt(packed):
        query_rows, positions, new_rows, cache_rows, length = packed
        key_rows = jnp.concatenate([cache_rows[:, 0], new_rows[:, 0]], axis=0)
        value_rows = jnp.concatenate([cache_rows[:, 1], new_rows[:, 1]], axis=0)
        allowed = jnp.where(
            column[None, :] < PMAX,
            column[None, :] < length,
            column[None, :] - PMAX <= positions[:, None],
        )

        def one_head(query_head):
            return softmax_mix(query_head, key_rows, value_rows, allowed, score_scale)

        mixed = lax.map(one_head, jnp.transpose(query_rows, (1, 0, 2)))
        return jnp.transpose(mixed, (1, 0, 2)).reshape(query_rows_all, heads_dev * HS)

    outputs = lax.map(prompt, (query_blocks, query_pos, new_blocks, cached, prefix_len))
    outputs = outputs.reshape(tp_count, rows_src, heads_dev * HS)
    attended = lax.all_to_all(outputs, "tp", split_axis=0, concat_axis=2, tiled=True).reshape(
        rows_src, HEADS * HS
    )
    capacity = max(rows_src // dev_count + 1, 2)
    width = new_kv.shape[1]
    spots = jnp.arange(rows_src)
    same_owner = (owner[:, None] == owner[None, :]) & (spots[None, :] < spots[:, None])
    within = jnp.sum(same_owner.astype(jnp.int32), axis=1)
    flat_index = owner * capacity + within
    send_rows = jnp.zeros((dev_count * capacity, width), jnp.bfloat16).at[flat_index].set(new_kv)
    send_slots = jnp.full((dev_count * capacity,), -1, jnp.int32).at[flat_index].set(slot)
    rows_in, slots_in = (
        lax.all_to_all(
            send_rows.reshape(dev_count, capacity, width),
            ("tp", "sub"),
            split_axis=0,
            concat_axis=0,
            tiled=True,
        ),
        lax.all_to_all(
            send_slots.reshape(dev_count, capacity),
            ("tp", "sub"),
            split_axis=0,
            concat_axis=0,
            tiled=True,
        ),
    )
    slots_flat = slots_in.reshape(-1)
    target = jnp.where(slots_flat >= 0, slots_flat, rows_src)
    pages = (
        jnp.zeros((rows_src, width), jnp.bfloat16)
        .at[target]
        .set(rows_in.reshape(-1, width), mode="drop")
    )
    return (attended, pages)


LOG2E = 1.4426950408889634


def attend_kernel(
    q_ref, new_ref, prefix_ref, bias_ref, o_ref,
    kv, news, acc, m_s, edge, send_sem, ici_sem, sib_sem, new_sem, newsib_sem, local_sem,
):
    t = lax.axis_index("tp")
    s = lax.axis_index("sub")
    h = t // 4
    y = t % 2
    zl = (t // 2) % 2
    inner = (h + zl) == 1
    outer = (h + zl) != 1
    zp = t + 2 - 4 * zl
    yp = t + 1 - 2 * y
    dp = zp + 1 - 2 * y
    sp = 1 - s
    near = 4 + y - 2 * h
    far = 6 * (1 - h) + y
    near_y = near + 1 - 2 * y
    far_y = far + 1 - 2 * y
    rows = new_ref.shape[0]
    shard = prefix_ref.shape[1]
    half = shard // 2
    me = (t % 4) * 2 + s

    def dev(tp, sub):
        return {"tp": tp, "sub": sub}

    barrier = pltpu.get_barrier_semaphore()
    for target in (dev(zp, s), dev(yp, s), dev(dp, s), dev(t, sp), dev(near, s)):
        pl.semaphore_signal(barrier, inc=1, device_id=target, device_id_type=pl.DeviceIdType.MESH)

    @pl.when(inner)
    def _():
        pl.semaphore_signal(
            barrier, inc=1, device_id=dev(far, s), device_id_type=pl.DeviceIdType.MESH
        )
        pl.semaphore_wait(barrier, 6)

    @pl.when(outer)
    def _():
        pl.semaphore_wait(barrier, 5)

    def copy(src, dst, slot, recv, target):
        return pltpu.make_async_remote_copy(
            src_ref=src, dst_ref=dst, send_sem=send_sem.at[slot], recv_sem=recv,
            device_id=target, device_id_type=pl.DeviceIdType.MESH,
        )

    def piece(src, part):
        return kv.at[src, pl.ds(pl.multiple_of(part * half, half), half)]

    def own_piece(prompt):
        return prefix_ref.at[prompt, pl.ds(pl.multiple_of(s * half, half), half)]

    def new_of(tp, sub):
        return news.at[(tp % 4) * 2 + sub]

    first = [
        copy(new_ref, new_of(t, s), 0, new_sem.at[0], dev(zp, s)),
        copy(new_ref, new_of(t, s), 1, new_sem.at[1], dev(yp, s)),
        copy(new_ref, new_of(t, s), 2, new_sem.at[2], dev(dp, s)),
        copy(new_ref, new_of(t, s), 3, newsib_sem.at[3], dev(t, sp)),
        copy(own_piece(h), piece(t, s), 4, ici_sem.at[0], dev(zp, s)),
        copy(own_piece(h), piece(t, s), 5, ici_sem.at[3], dev(yp, s)),
    ]
    load = pltpu.make_async_copy(prefix_ref.at[h], kv.at[t], local_sem.at[0])
    load.start()
    keep = pltpu.make_async_copy(new_ref, news.at[me], local_sem.at[1])
    keep.start()
    for one in first:
        one.start()
    cross_near = copy(own_piece(1 - h), piece(t, s), 6, ici_sem.at[1], dev(near, s))
    cross_far = copy(own_piece(1 - h), piece(t, s), 6, ici_sem.at[2], dev(near, s))
    pl.when(inner)(cross_near.start)
    pl.when(outer)(cross_far.start)

    def to_sib(role, src):
        return copy(piece(src, s), piece(src, s), 8 + role, sib_sem.at[role], dev(t, sp))

    def to_y(role, src):
        return copy(piece(src, s), piece(src, s), 16 + role, ici_sem.at[4 + role], dev(yp, s))

    def to_z(role, src):
        return copy(piece(src, s), piece(src, s), 20 + role, ici_sem.at[role], dev(zp, s))

    def new_sib(role, tp):
        return copy(new_of(tp, s), new_of(tp, s), 24 + role, newsib_sem.at[role], dev(t, sp))

    def got(role, src):
        copy(piece(src, s), piece(src, s), 31, ici_sem.at[role], dev(t, sp)).wait_recv()

    def got_sib(role, src):
        copy(piece(src, sp), piece(src, sp), 31, sib_sem.at[role], dev(t, sp)).wait_recv()

    def column(role, src):
        got(role, src)
        to_y(role, src).start()
        to_sib(role, src).start()

    def across(role, src):
        got(role, src)
        to_sib(role, src).start()

    def column_inner(role, src):
        got(role, src)
        to_z(role, src).start()
        to_y(role, src).start()
        to_sib(role, src).start()

    scale = HS ** (-0.5) * LOG2E
    group = HEADS // KVH

    def attend(pieces, bias, start, actions=()):
        def key_head(g, carry):
            for step, condition, action in actions:
                @pl.when((g == step) if condition is None else ((g == step) & condition))
                def _():
                    action()
            key_cols = pl.ds(pl.multiple_of(g * HS, HS), HS)
            value_cols = pl.ds(pl.multiple_of((KVH + g) * HS, HS), HS)
            keys = jnp.concatenate([load_cols(key_cols) for load_cols in pieces], axis=0)
            values = jnp.concatenate([load_cols(value_cols) for load_cols in pieces], axis=0)
            values = jnp.concatenate([values, jnp.ones_like(values)], axis=1)
            offset = bias()
            for i in range(group):
                at = pl.ds(pl.multiple_of((g * group + i) * HS, HS), HS)
                at_row = pl.ds(pl.multiple_of((g * group + i) * rows, rows), rows)
                scores = lax.dot_general(
                    q_ref[:, at], keys, (((1,), (1,)), ((), ())), preferred_element_type=jnp.float32
                )
                scores = scores * scale + offset
                top = jnp.max(scores, axis=1, keepdims=True)
                if start:
                    best = jnp.broadcast_to(top, (rows, HS))
                else:
                    old = m_s[at_row, :]
                    best = jnp.maximum(old, top)
                weights = jnp.exp2(scores - best[:, :1]).astype(jnp.bfloat16)
                mixed = jnp.dot(weights, values, preferred_element_type=jnp.float32)
                if start:
                    acc[at_row, :] = mixed
                else:
                    fade = jnp.exp2(old - best)
                    acc[at_row, :] = acc[at_row, :] * jnp.concatenate([fade, fade], axis=1) + mixed
                m_s[at_row, :] = best
            return carry

        lax.fori_loop(0, KVH, key_head, 0)

    def shard_cols(src):
        return lambda cols: kv[src, :, cols]

    def shard_bias(src):
        return bias_ref[:, pl.ds(pl.multiple_of(src * shard, shard), shard)]

    def pair_bias(a, b):
        return lambda: jnp.concatenate([shard_bias(a), shard_bias(b)], axis=1)

    causal = lax.broadcasted_iota(jnp.int32, (rows, rows), 1) <= lax.broadcasted_iota(
        jnp.int32, (rows, rows), 0
    )
    edge[:, :rows] = jnp.where(causal, 0.0, -1e30)
    edge[:, rows:] = jnp.broadcast_to(shard_bias(t), (rows, shard))
    load.wait()
    attend([lambda cols: new_ref[:, cols], shard_cols(t)], lambda: edge[...], True)

    for role, tp in enumerate((zp, yp, dp)):
        copy(new_of(tp, s), new_of(tp, s), 31, new_sem.at[role], dev(t, sp)).wait_recv()
        new_sib(role, tp).start()
    keep.wait()
    for role, tp in enumerate((zp, yp, dp, t)):
        copy(new_of(tp, sp), new_of(tp, sp), 31, newsib_sem.at[role], dev(t, sp)).wait_recv()
    count = news.shape[0]
    earlier = lax.broadcasted_iota(jnp.int32, (1, count * rows), 1) < me * rows
    new_bias = jnp.where(earlier, 0.0, -1e30)

    def arrive_first():
        column(0, zp)
        across(3, yp)

    attend(
        [lambda cols, i=i: news[i, :, cols] for i in range(count)], lambda: new_bias, False,
        [(7, None, arrive_first), (7, inner, lambda: column_inner(1, near))],
    )
    got_sib(0, zp)
    got_sib(3, yp)
    attend(
        [shard_cols(zp), shard_cols(yp)], pair_bias(zp, yp), False,
        [
            (4, inner, lambda: column_inner(2, far)),
            (7, outer, lambda: column(1, near)),
            (7, None, lambda: across(4, dp)),
        ],
    )
    got_sib(4, dp)
    got_sib(1, near)
    attend(
        [shard_cols(dp), shard_cols(near)], pair_bias(dp, near), False,
        [
            (6, outer, lambda: column(2, far)),
            (7, None, lambda: across(5, near_y)),
        ],
    )
    got_sib(5, near_y)
    got_sib(2, far)
    attend(
        [shard_cols(near_y), shard_cols(far)], pair_bias(near_y, far), False,
        [(6, None, lambda: across(6, far_y))],
    )
    got_sib(6, far_y)
    attend([shard_cols(far_y)], lambda: shard_bias(far_y), False)

    def finish(i, carry):
        at = pl.ds(pl.multiple_of(i * HS, HS), HS)
        at_row = pl.ds(pl.multiple_of(i * rows, rows), rows)
        o_ref[:, at] = (acc[at_row, :HS] / acc[at_row, HS:]).astype(o_ref.dtype)
        return carry

    lax.fori_loop(0, HEADS, finish, 0)

    for one in first:
        one.wait_send()
    cross_near.wait_send()
    for role, src in enumerate((zp, near, far, yp, dp, near_y, far_y)):
        to_sib(role, src).wait_send()
    for role, src in enumerate((zp, near, far)):
        to_y(role, src).wait_send()
    for role, tp in enumerate((zp, yp, dp)):
        new_sib(role, tp).wait_send()

    @pl.when(inner)
    def _():
        to_z(1, near).wait_send()
        to_z(2, far).wait_send()


def send_pages(new_kv, owner, slot):
    dev_count = lax.axis_size("tp") * lax.axis_size("sub")
    rows, width = new_kv.shape
    capacity = max(rows // dev_count + 1, 2)
    spots = jnp.arange(rows)
    same_owner = (owner[:, None] == owner[None, :]) & (spots[None, :] < spots[:, None])
    within = jnp.sum(same_owner.astype(jnp.int32), axis=1)
    flat_index = owner * capacity + within
    places = jnp.arange(dev_count * capacity)
    pick = (places[:, None] == flat_index[None, :]).astype(jnp.bfloat16)
    marks = jnp.broadcast_to((slot + 1).astype(jnp.bfloat16)[:, None], (rows, HS))
    packed = jnp.concatenate([new_kv, marks], axis=1)
    sent = jnp.dot(pick, packed, preferred_element_type=jnp.float32).astype(jnp.bfloat16)
    rows_in = lax.all_to_all(
        sent.reshape(dev_count, capacity, width + HS),
        ("tp", "sub"), split_axis=0, concat_axis=0, tiled=True,
    ).reshape(dev_count * capacity, width + HS)
    slots_in = rows_in[:, width].astype(jnp.int32) - 1
    put = (jnp.arange(rows)[:, None] == slots_in[None, :]).astype(jnp.bfloat16)
    return jnp.dot(put, rows_in[:, :width], preferred_element_type=jnp.float32).astype(jnp.bfloat16)


def fused(queries, new_kv, prefix_kv, prefix_len, owner, slot):
    rows = queries.shape[0]
    shard = prefix_kv.shape[1]
    length = prefix_len[lax.axis_index("tp") // 4]
    bias = jnp.where(jnp.arange(PMAX)[None, :] < length, 0.0, -1e30).astype(jnp.float32)
    pages = send_pages(new_kv, owner, slot)
    vmem = pl.BlockSpec(memory_space=pltpu.VMEM)
    attended = pl.pallas_call(
        attend_kernel,
        out_shape=jax.ShapeDtypeStruct(queries.shape, jnp.bfloat16),
        in_specs=[vmem, vmem, pl.BlockSpec(memory_space=pl.ANY), vmem],
        out_specs=vmem,
        scratch_shapes=[
            pltpu.VMEM((PMAX // shard, shard, new_kv.shape[1]), jnp.bfloat16),
            pltpu.VMEM((SPAN // rows, rows, new_kv.shape[1]), jnp.bfloat16),
            pltpu.VMEM((HEADS * rows, 2 * HS), jnp.float32),
            pltpu.VMEM((HEADS * rows, HS), jnp.float32),
            pltpu.VMEM((rows, rows + shard), jnp.float32),
            pltpu.SemaphoreType.DMA((32,)),
            pltpu.SemaphoreType.DMA((7,)),
            pltpu.SemaphoreType.DMA((7,)),
            pltpu.SemaphoreType.DMA((3,)),
            pltpu.SemaphoreType.DMA((4,)),
            pltpu.SemaphoreType.DMA((2,)),
        ],
        compiler_params=pltpu.CompilerParams(
            collective_id=0, has_side_effects=True, vmem_limit_bytes=60 * 2**20
        ),
        cost_estimate=pl.CostEstimate(
            flops=4 * rows * HEADS * HS * (PMAX + SPAN), bytes_accessed=2**23, transcendentals=0
        ),
        name="attend",
    )(queries, new_kv, prefix_kv, bias)
    return (attended, pages)


def solution(mesh):
    placed = (
        P(("groups", "tp", "sub"), None),
        P(("groups", "tp", "sub"), None),
        P("groups", "tp", None),
        P("groups"),
        P(("groups", "tp", "sub")),
        P(("groups", "tp", "sub")),
    )
    small = mesh.shape["tp"] == 8 and mesh.shape["sub"] == 2
    body = fused if small else shards
    return jax.shard_map(
        body,
        mesh=mesh,
        in_specs=placed,
        out_specs=(P(("groups", "tp", "sub"), None), P(("groups", "tp", "sub"), None)),
        check_vma=False,
    )
```

```python
import jax
import jax.numpy as jnp
import numpy as np
from jax import lax
from jax.experimental import pallas as pl
from jax.experimental.pallas import tpu as pltpu
from jax.sharding import PartitionSpec as P

HEADS = 96
KVH = 8
HS = 128
SPAN = 1024
PMAX = 4096


def softmax_mix(query_head, key_head, value_head, allowed, score_scale):
    scores = jnp.dot(query_head, key_head.T, preferred_element_type=jnp.float32) * score_scale
    scores = jnp.where(allowed, scores, -1e30)
    top_score = jnp.max(scores, axis=1, keepdims=True)
    expo = jnp.where(allowed, jnp.exp(scores - top_score), 0.0)
    total = jnp.sum(expo, axis=1, keepdims=True)
    weights = (expo / total).astype(jnp.bfloat16)
    return jnp.dot(weights, value_head, preferred_element_type=jnp.float32).astype(jnp.bfloat16)


def shards(queries, new_kv, prefix_kv, prefix_len, owner, slot):
    tp_count = lax.axis_size("tp")
    sub_count = lax.axis_size("sub")
    sub_index = lax.axis_index("sub")
    dev_count = tp_count * sub_count
    rows_src = queries.shape[0]
    prompts = prefix_len.shape[0]
    heads_dev = HEADS // tp_count
    group_size = HEADS // KVH
    score_scale = HS ** (-0.5)
    head_of_peer = np.arange(tp_count) * heads_dev // group_size
    kv_local = new_kv.reshape(rows_src, 2, KVH, HS)
    query_send = queries.reshape(rows_src, tp_count, heads_dev * HS)
    query_recv = lax.all_to_all(query_send, "tp", split_axis=1, concat_axis=0, tiled=True)
    dest_heads = np.repeat(head_of_peer, sub_count)
    key_send = jnp.take(kv_local, dest_heads, axis=2)
    key_send = jnp.transpose(key_send, (2, 0, 1, 3)).reshape(dev_count, rows_src, 2 * HS)
    new_keys = lax.all_to_all(
        key_send, ("tp", "sub"), split_axis=0, concat_axis=0, tiled=True
    ).reshape(-1, 2 * HS)
    shard_rows = prefix_kv.shape[1]
    cache_local = prefix_kv.reshape(prompts, shard_rows, 2, KVH, HS)
    prefix_send = jnp.take(cache_local, head_of_peer, axis=3)
    prefix_send = jnp.transpose(prefix_send, (0, 3, 1, 2, 4)).reshape(
        prompts, tp_count, shard_rows, 2 * HS
    )
    cached = lax.all_to_all(prefix_send, "tp", split_axis=1, concat_axis=1, tiled=True)
    cached = cached.reshape(prompts, PMAX, 2, HS)
    local_rows = tp_count * rows_src
    query_rows_all = local_rows // prompts
    arrival = jnp.arange(local_rows)
    global_row = (arrival // rows_src * sub_count + sub_index) * rows_src + arrival % rows_src
    query_pos = (global_row % SPAN).reshape(prompts, query_rows_all)
    query_blocks = query_recv.reshape(prompts, query_rows_all, heads_dev, HS)
    new_blocks = new_keys.reshape(prompts, SPAN, 2, HS)
    column = jnp.arange(PMAX + SPAN)

    def prompt(packed):
        query_rows, positions, new_rows, cache_rows, length = packed
        key_rows = jnp.concatenate([cache_rows[:, 0], new_rows[:, 0]], axis=0)
        value_rows = jnp.concatenate([cache_rows[:, 1], new_rows[:, 1]], axis=0)
        allowed = jnp.where(
            column[None, :] < PMAX,
            column[None, :] < length,
            column[None, :] - PMAX <= positions[:, None],
        )

        def one_head(query_head):
            return softmax_mix(query_head, key_rows, value_rows, allowed, score_scale)

        mixed = lax.map(one_head, jnp.transpose(query_rows, (1, 0, 2)))
        return jnp.transpose(mixed, (1, 0, 2)).reshape(query_rows_all, heads_dev * HS)

    outputs = lax.map(prompt, (query_blocks, query_pos, new_blocks, cached, prefix_len))
    outputs = outputs.reshape(tp_count, rows_src, heads_dev * HS)
    attended = lax.all_to_all(outputs, "tp", split_axis=0, concat_axis=2, tiled=True).reshape(
        rows_src, HEADS * HS
    )
    capacity = max(rows_src // dev_count + 1, 2)
    width = new_kv.shape[1]
    spots = jnp.arange(rows_src)
    same_owner = (owner[:, None] == owner[None, :]) & (spots[None, :] < spots[:, None])
    within = jnp.sum(same_owner.astype(jnp.int32), axis=1)
    flat_index = owner * capacity + within
    send_rows = jnp.zeros((dev_count * capacity, width), jnp.bfloat16).at[flat_index].set(new_kv)
    send_slots = jnp.full((dev_count * capacity,), -1, jnp.int32).at[flat_index].set(slot)
    rows_in, slots_in = (
        lax.all_to_all(
            send_rows.reshape(dev_count, capacity, width),
            ("tp", "sub"),
            split_axis=0,
            concat_axis=0,
            tiled=True,
        ),
        lax.all_to_all(
            send_slots.reshape(dev_count, capacity),
            ("tp", "sub"),
            split_axis=0,
            concat_axis=0,
            tiled=True,
        ),
    )
    slots_flat = slots_in.reshape(-1)
    target = jnp.where(slots_flat >= 0, slots_flat, rows_src)
    pages = (
        jnp.zeros((rows_src, width), jnp.bfloat16)
        .at[target]
        .set(rows_in.reshape(-1, width), mode="drop")
    )
    return (attended, pages)


LOG2E = 1.4426950408889634


def attend_kernel(
    q_ref, new_ref, prefix_ref, bias_ref, o_ref,
    kv, news, acc, m_s, edge, send_sem, ici_sem, sib_sem, new_sem, newsib_sem, local_sem,
):
    t = lax.axis_index("tp")
    s = lax.axis_index("sub")
    h = t // 4
    y = t % 2
    zl = (t // 2) % 2
    inner = (h + zl) == 1
    outer = (h + zl) != 1
    zp = t + 2 - 4 * zl
    yp = t + 1 - 2 * y
    dp = zp + 1 - 2 * y
    sp = 1 - s
    near = 4 + y - 2 * h
    far = 6 * (1 - h) + y
    near_y = near + 1 - 2 * y
    far_y = far + 1 - 2 * y
    rows = new_ref.shape[0]
    shard = prefix_ref.shape[1]
    half = shard // 2
    me = (t % 4) * 2 + s

    def dev(tp, sub):
        return {"tp": tp, "sub": sub}

    barrier = pltpu.get_barrier_semaphore()
    for target in (dev(zp, s), dev(yp, s), dev(dp, s), dev(t, sp), dev(near, s)):
        pl.semaphore_signal(barrier, inc=1, device_id=target, device_id_type=pl.DeviceIdType.MESH)

    @pl.when(inner)
    def _():
        pl.semaphore_signal(
            barrier, inc=1, device_id=dev(far, s), device_id_type=pl.DeviceIdType.MESH
        )
        pl.semaphore_wait(barrier, 6)

    @pl.when(outer)
    def _():
        pl.semaphore_wait(barrier, 5)

    def copy(src, dst, slot, recv, target):
        return pltpu.make_async_remote_copy(
            src_ref=src, dst_ref=dst, send_sem=send_sem.at[slot], recv_sem=recv,
            device_id=target, device_id_type=pl.DeviceIdType.MESH,
        )

    def piece(src, part):
        return kv.at[src, pl.ds(pl.multiple_of(part * half, half), half)]

    def own_piece(prompt):
        return prefix_ref.at[prompt, pl.ds(pl.multiple_of(s * half, half), half)]

    def new_of(tp, sub):
        return news.at[(tp % 4) * 2 + sub]

    first = [
        copy(new_ref, new_of(t, s), 0, new_sem.at[0], dev(zp, s)),
        copy(new_ref, new_of(t, s), 1, new_sem.at[1], dev(yp, s)),
        copy(new_ref, new_of(t, s), 2, new_sem.at[2], dev(dp, s)),
        copy(new_ref, new_of(t, s), 3, newsib_sem.at[3], dev(t, sp)),
        copy(own_piece(h), piece(t, s), 4, ici_sem.at[0], dev(zp, s)),
        copy(own_piece(h), piece(t, s), 5, ici_sem.at[3], dev(yp, s)),
    ]
    load = pltpu.make_async_copy(prefix_ref.at[h], kv.at[t], local_sem.at[0])
    load.start()
    keep = pltpu.make_async_copy(new_ref, news.at[me], local_sem.at[1])
    keep.start()
    for one in first:
        one.start()
    cross_near = copy(own_piece(1 - h), piece(t, s), 6, ici_sem.at[1], dev(near, s))
    cross_far = copy(own_piece(1 - h), piece(t, s), 6, ici_sem.at[2], dev(near, s))
    pl.when(inner)(cross_near.start)
    pl.when(outer)(cross_far.start)

    def to_sib(role, src):
        return copy(piece(src, s), piece(src, s), 8 + role, sib_sem.at[role], dev(t, sp))

    def to_y(role, src):
        return copy(piece(src, s), piece(src, s), 16 + role, ici_sem.at[4 + role], dev(yp, s))

    def to_z(role, src):
        return copy(piece(src, s), piece(src, s), 20 + role, ici_sem.at[role], dev(zp, s))

    def pass_z(role, src):
        return copy(piece(src, s), piece(src, s), 27, ici_sem.at[role], dev(zp, s))

    def new_sib(role, tp):
        return copy(new_of(tp, s), new_of(tp, s), 24 + role, newsib_sem.at[role], dev(t, sp))

    def got(role, src):
        copy(piece(src, s), piece(src, s), 31, ici_sem.at[role], dev(t, sp)).wait_recv()

    def got_sib(role, src):
        copy(piece(src, sp), piece(src, sp), 31, sib_sem.at[role], dev(t, sp)).wait_recv()

    def column(role, src):
        got(role, src)
        to_y(role, src).start()
        to_sib(role, src).start()

    def across(role, src):
        got(role, src)
        to_sib(role, src).start()

    def column_inner(role, src):
        got(role, src)
        to_z(role, src).start()
        to_y(role, src).start()
        to_sib(role, src).start()

    scale = HS ** (-0.5) * LOG2E
    group = HEADS // KVH

    def attend(pieces, bias, start, actions=()):
        def key_head(g, carry):
            for step, condition, action in actions:
                @pl.when((g == step) if condition is None else ((g == step) & condition))
                def _():
                    action()
            key_cols = pl.ds(pl.multiple_of(g * HS, HS), HS)
            value_cols = pl.ds(pl.multiple_of((KVH + g) * HS, HS), HS)
            keys = jnp.concatenate([load_cols(key_cols) for load_cols in pieces], axis=0)
            values = jnp.concatenate([load_cols(value_cols) for load_cols in pieces], axis=0)
            values = jnp.concatenate([values, jnp.ones_like(values)], axis=1)
            offset = bias()
            for i in range(group):
                at = pl.ds(pl.multiple_of((g * group + i) * HS, HS), HS)
                at_row = pl.ds(pl.multiple_of((g * group + i) * rows, rows), rows)
                scores = lax.dot_general(
                    q_ref[:, at], keys, (((1,), (1,)), ((), ())), preferred_element_type=jnp.float32
                )
                scores = scores * scale + offset
                top = jnp.max(scores, axis=1, keepdims=True)
                if start:
                    best = jnp.broadcast_to(top, (rows, HS))
                else:
                    old = m_s[at_row, :]
                    best = jnp.maximum(old, top)
                weights = jnp.exp2(scores - best[:, :1]).astype(jnp.bfloat16)
                mixed = jnp.dot(weights, values, preferred_element_type=jnp.float32)
                if start:
                    acc[at_row, :] = mixed
                else:
                    fade = jnp.exp2(old - best)
                    acc[at_row, :] = acc[at_row, :] * jnp.concatenate([fade, fade], axis=1) + mixed
                m_s[at_row, :] = best
            return carry

        lax.fori_loop(0, KVH, key_head, 0)

    def shard_cols(src):
        return lambda cols: kv[src, :, cols]

    def shard_bias(src):
        return bias_ref[:, pl.ds(pl.multiple_of(src * shard, shard), shard)]

    def pair_bias(a, b):
        return lambda: jnp.concatenate([shard_bias(a), shard_bias(b)], axis=1)

    causal = lax.broadcasted_iota(jnp.int32, (rows, rows), 1) <= lax.broadcasted_iota(
        jnp.int32, (rows, rows), 0
    )
    edge[:, :rows] = jnp.where(causal, 0.0, -1e30)
    edge[:, rows:] = jnp.broadcast_to(shard_bias(t), (rows, shard))
    load.wait()
    attend([lambda cols: new_ref[:, cols], shard_cols(t)], lambda: edge[...], True)

    for role, tp in enumerate((zp, yp, dp)):
        copy(new_of(tp, s), new_of(tp, s), 31, new_sem.at[role], dev(t, sp)).wait_recv()
        new_sib(role, tp).start()
    keep.wait()
    for role, tp in enumerate((zp, yp, dp, t)):
        copy(new_of(tp, sp), new_of(tp, sp), 31, newsib_sem.at[role], dev(t, sp)).wait_recv()
    count = news.shape[0]
    earlier = lax.broadcasted_iota(jnp.int32, (1, count * rows), 1) < me * rows
    new_bias = jnp.where(earlier, 0.0, -1e30)

    def first_inner():
        across(0, zp)
        across(3, yp)

    def first_outer():
        column(0, zp)
        got(3, yp)
        pass_z(4, yp).start()
        to_sib(3, yp).start()

    def last_inner():
        got(6, far_y)
        pass_z(6, far_y).start()
        to_sib(6, far_y).start()

    attend(
        [lambda cols, i=i: news[i, :, cols] for i in range(count)], lambda: new_bias, False,
        [(7, inner, first_inner), (7, outer, first_outer), (7, inner, lambda: column_inner(1, near))],
    )
    got_sib(0, zp)
    got_sib(3, yp)
    attend(
        [shard_cols(zp), shard_cols(yp)], pair_bias(zp, yp), False,
        [
            (4, inner, lambda: column_inner(2, far)),
            (7, outer, lambda: column(1, near)),
            (7, None, lambda: across(4, dp)),
        ],
    )
    got_sib(4, dp)
    got_sib(1, near)
    attend(
        [shard_cols(dp), shard_cols(near)], pair_bias(dp, near), False,
        [
            (6, outer, lambda: across(2, far)),
            (7, None, lambda: across(5, near_y)),
            (7, inner, last_inner),
        ],
    )
    got_sib(5, near_y)
    got_sib(2, far)
    attend(
        [shard_cols(near_y), shard_cols(far)], pair_bias(near_y, far), False,
        [(6, outer, lambda: across(6, far_y))],
    )
    got_sib(6, far_y)
    attend([shard_cols(far_y)], lambda: shard_bias(far_y), False)

    def finish(i, carry):
        at = pl.ds(pl.multiple_of(i * HS, HS), HS)
        at_row = pl.ds(pl.multiple_of(i * rows, rows), rows)
        o_ref[:, at] = (acc[at_row, :HS] / acc[at_row, HS:]).astype(o_ref.dtype)
        return carry

    lax.fori_loop(0, HEADS, finish, 0)

    for one in first:
        one.wait_send()
    cross_near.wait_send()
    for role, src in enumerate((zp, near, far, yp, dp, near_y, far_y)):
        to_sib(role, src).wait_send()
    to_y(1, near).wait_send()
    for role, tp in enumerate((zp, yp, dp)):
        new_sib(role, tp).wait_send()

    @pl.when(inner)
    def _():
        to_z(1, near).wait_send()
        to_z(2, far).wait_send()
        to_y(2, far).wait_send()
        pass_z(6, far_y).wait_send()

    @pl.when(outer)
    def _():
        to_y(0, zp).wait_send()
        pass_z(4, yp).wait_send()


def send_pages(new_kv, owner, slot):
    dev_count = lax.axis_size("tp") * lax.axis_size("sub")
    rows, width = new_kv.shape
    capacity = max(rows // dev_count + 1, 2)
    spots = jnp.arange(rows)
    same_owner = (owner[:, None] == owner[None, :]) & (spots[None, :] < spots[:, None])
    within = jnp.sum(same_owner.astype(jnp.int32), axis=1)
    flat_index = owner * capacity + within
    places = jnp.arange(dev_count * capacity)
    pick = (places[:, None] == flat_index[None, :]).astype(jnp.bfloat16)
    marks = jnp.broadcast_to((slot + 1).astype(jnp.bfloat16)[:, None], (rows, HS))
    packed = jnp.concatenate([new_kv, marks], axis=1)
    sent = jnp.dot(pick, packed, preferred_element_type=jnp.float32).astype(jnp.bfloat16)
    rows_in = lax.all_to_all(
        sent.reshape(dev_count, capacity, width + HS),
        ("tp", "sub"), split_axis=0, concat_axis=0, tiled=True,
    ).reshape(dev_count * capacity, width + HS)
    slots_in = rows_in[:, width].astype(jnp.int32) - 1
    put = (jnp.arange(rows)[:, None] == slots_in[None, :]).astype(jnp.bfloat16)
    return jnp.dot(put, rows_in[:, :width], preferred_element_type=jnp.float32).astype(jnp.bfloat16)


def fused(queries, new_kv, prefix_kv, prefix_len, owner, slot):
    rows = queries.shape[0]
    shard = prefix_kv.shape[1]
    length = prefix_len[lax.axis_index("tp") // 4]
    bias = jnp.where(jnp.arange(PMAX)[None, :] < length, 0.0, -1e30).astype(jnp.float32)
    pages = send_pages(new_kv, owner, slot)
    vmem = pl.BlockSpec(memory_space=pltpu.VMEM)
    attended = pl.pallas_call(
        attend_kernel,
        out_shape=jax.ShapeDtypeStruct(queries.shape, jnp.bfloat16),
        in_specs=[vmem, vmem, pl.BlockSpec(memory_space=pl.ANY), vmem],
        out_specs=vmem,
        scratch_shapes=[
            pltpu.VMEM((PMAX // shard, shard, new_kv.shape[1]), jnp.bfloat16),
            pltpu.VMEM((SPAN // rows, rows, new_kv.shape[1]), jnp.bfloat16),
            pltpu.VMEM((HEADS * rows, 2 * HS), jnp.float32),
            pltpu.VMEM((HEADS * rows, HS), jnp.float32),
            pltpu.VMEM((rows, rows + shard), jnp.float32),
            pltpu.SemaphoreType.DMA((32,)),
            pltpu.SemaphoreType.DMA((7,)),
            pltpu.SemaphoreType.DMA((7,)),
            pltpu.SemaphoreType.DMA((3,)),
            pltpu.SemaphoreType.DMA((4,)),
            pltpu.SemaphoreType.DMA((2,)),
        ],
        compiler_params=pltpu.CompilerParams(
            collective_id=0, has_side_effects=True, vmem_limit_bytes=60 * 2**20
        ),
        cost_estimate=pl.CostEstimate(
            flops=4 * rows * HEADS * HS * (PMAX + SPAN), bytes_accessed=2**23, transcendentals=0
        ),
        name="attend",
    )(queries, new_kv, prefix_kv, bias)
    return (attended, pages)


def solution(mesh):
    placed = (
        P(("groups", "tp", "sub"), None),
        P(("groups", "tp", "sub"), None),
        P("groups", "tp", None),
        P("groups"),
        P(("groups", "tp", "sub")),
        P(("groups", "tp", "sub")),
    )
    small = mesh.shape["tp"] == 8 and mesh.shape["sub"] == 2
    body = fused if small else shards
    return jax.shard_map(
        body,
        mesh=mesh,
        in_specs=placed,
        out_specs=(P(("groups", "tp", "sub"), None), P(("groups", "tp", "sub"), None)),
        check_vma=False,
    )
```
